32 devices in a mesh: seq: 8 (over y, x, core), chan: 4 (over z).
Axes of the slice: x: 2, y: 2, z: 4, core: 2. Of those that a mesh axis runs over, the one named last changes fastest.
Arguments:
- gate_in: bfloat16 [4096, 1024], P('seq', 'chan'), may hold values from -6 to 6
- out_gate: bfloat16 [4096, 1024], P('seq', 'chan'), may hold values from -6 to 6
- value_in: bfloat16 [4096, 1024], P('seq', 'chan'), may hold values from -6 to 6
- out_grad: bfloat16 [4096, 1024], P('seq', 'chan'), may hold values from -6 to 6
- skip_gain: float32 [1024], P('chan'), may hold values from -1 to 1
- filter_taps: float32 [4096, 256], P('seq'), may hold values from -0.09375 to 0.09375
Outputs:
- grad_gate: bfloat16 [4096, 1024], P('seq', 'chan')
- grad_out_gate: bfloat16 [4096, 1024], P('seq', 'chan')
- grad_value: bfloat16 [4096, 1024], P('seq', 'chan')
- skip_grad: float32 [1024], P('chan')
- taps_grad: float32 [4096, 256], P('seq')
The draws below stay inside these ranges and needn't reach their ends.
All inputs are finite; a program needn't handle non-finite values.
Results may differ from the reference program's by a relative error of at most 0.0052.
Values sent between devices are 32-bit elements; how exact they have to be, the bound alone decides.
A program may use at most 128 MiB of HBM per device.

```python
import jax
import jax.numpy as jnp
from jax import lax

SEQ = 4096
CHANNELS = 1024
FILTERS = 256


def shard_levels(stream_key, extent, shards, smallest, top_value):
    level, own = 1.0, jax.random.fold_in(stream_key, 6)
    for axis_at, parts in shards:
        steps = jnp.exp(jax.random.uniform(jax.random.fold_in(own, axis_at), (parts,), jnp.float32, smallest / len(shards), top_value / len(shards)))
        level = level * jnp.repeat(steps, extent[axis_at] // parts).reshape([-1 if axis == axis_at else 1 for axis in range(len(extent))])
    return level


def centred(rng, extent, scale, limit, split=(), kind=jnp.bfloat16):
    array = scale * jax.random.normal(rng, extent, jnp.float32)
    if split:
        array = array * shard_levels(rng, extent, split, -0.22, 0.18)
    return jnp.clip(array, -limit, limit).astype(kind)


def setup_inputs(seed: int = 0) -> dict:
    streams_of = jax.random.split(jax.random.key(seed), 7)
    gate_in = centred(streams_of[0], (SEQ, CHANNELS), 1.0, 6.0, ((0, 8), (1, 4)))
    out_gate = centred(streams_of[1], (SEQ, CHANNELS), 1.0, 6.0, ((0, 8), (1, 4)))
    value_in = centred(streams_of[2], (SEQ, CHANNELS), 1.0, 6.0, ((0, 8), (1, 4)))
    out_grad = centred(streams_of[3], (SEQ, CHANNELS), 1.0, 6.0, ((0, 8), (1, 4)))
    skip_gain = jnp.clip(jax.random.uniform(streams_of[4], (CHANNELS,), jnp.float32, -1.0, 1.0) * shard_levels(streams_of[4], (CHANNELS,), ((0, 4),), -0.4, 0.0), -1.0, 1.0)
    filter_taps = centred(streams_of[5], (SEQ, FILTERS), SEQ ** -0.5, 0.09375, ((0, 8),), jnp.float32)
    return dict(gate_in=gate_in, out_gate=out_gate, value_in=value_in, out_grad=out_grad, skip_gain=skip_gain, filter_taps=filter_taps)


def reference(gate_in, out_gate, value_in, out_grad, skip_gain, filter_taps):
    copies = CHANNELS // FILTERS
    filt_all = jnp.tile(filter_taps, (1, copies))
    mixed_bf = lax.optimization_barrier((gate_in.astype(jnp.float32) * value_in.astype(jnp.float32)).astype(jnp.bfloat16))
    mixed_in = mixed_bf.astype(jnp.float32)
    gated_bf = lax.optimization_barrier((out_grad.astype(jnp.float32) * out_gate.astype(jnp.float32)).astype(jnp.bfloat16))
    gated_grad = gated_bf.astype(jnp.float32)
    padding = ((0, SEQ), (0, 0))
    spec_mixed = jnp.fft.fft(jnp.pad(mixed_in, padding), axis=0)
    spec_gated = jnp.fft.fft(jnp.pad(gated_grad, padding), axis=0)
    spec_filt = jnp.fft.fft(jnp.pad(filt_all, padding), axis=0)
    conv = jnp.real(jnp.fft.ifft(spec_filt * spec_mixed, axis=0)[:SEQ])
    corr = jnp.real(jnp.fft.ifft(spec_gated * jnp.conj(spec_filt), axis=0)[:SEQ])
    filt_grad = jnp.real(jnp.fft.ifft(spec_gated * jnp.conj(spec_mixed), axis=0)[:SEQ])
    out32 = out_grad.astype(jnp.float32)
    grad_out_gate = (out32 * (conv + skip_gain[None] * mixed_in)).astype(jnp.bfloat16)
    mix_grad = corr + skip_gain[None] * gated_grad
    grad_gate = (mix_grad * value_in.astype(jnp.float32)).astype(jnp.bfloat16)
    grad_value = (mix_grad * gate_in.astype(jnp.float32)).astype(jnp.bfloat16)
    skip_grad = jnp.sum(gated_grad * mixed_in, axis=0)
    taps_grad = jnp.sum(filt_grad.reshape(SEQ, copies, FILTERS), axis=1)
    return grad_gate, grad_out_gate, grad_value, skip_grad, taps_grad
```

```python
import functools
import math

import jax
import jax.numpy as jnp
import numpy as np
from jax import lax
from jax.experimental import pallas as pl
from jax.experimental.pallas import tpu as pltpu
from jax.sharding import PartitionSpec as P

INNER = 256


def scaled(x, factor):
    if x is None or factor == 0.0:
        return None
    if factor == 1.0:
        return x
    if factor == -1.0:
        return -x
    return x * factor


def plus(a, b):
    if a is None:
        return b
    if b is None:
        return a
    return a + b


def minus(a, b):
    if b is None:
        return a
    if a is None:
        return -b
    return a - b


def turn(z, index, count, sign):
    re, im = z
    quarter = {0: (1.0, 0.0), 1: (0.0, 1.0), 2: (-1.0, 0.0), 3: (0.0, -1.0)}
    if 4 * index % count == 0:
        cos_v, sin_v = quarter[4 * index // count % 4]
    else:
        cos_v = math.cos(2.0 * math.pi * index / count)
        sin_v = math.sin(2.0 * math.pi * index / count)
    sin_v *= sign
    return (
        minus(scaled(re, cos_v), scaled(im, sin_v)),
        plus(scaled(im, cos_v), scaled(re, sin_v)),
    )


def small_rfft(rows):
    count = len(rows)
    if count == 1:
        return [(rows[0], None)]
    even = small_rfft(rows[0::2])
    odd = small_rfft(rows[1::2])
    out = [None] * (count // 2 + 1)
    for k in range(count // 4 + 1):
        t = turn(odd[k], k, count, -1.0)
        e = even[k]
        out[k] = (plus(e[0], t[0]), plus(e[1], t[1]))
        if count // 2 - k != k:
            out[count // 2 - k] = (minus(e[0], t[0]), minus(t[1], e[1]))
    return out


def small_irfft(spec, count):
    if count == 1:
        return [spec[0][0]]
    half = count // 2
    even, odd = [], []
    for k in range(count // 4 + 1):
        a, b = spec[k], spec[half - k]
        even.append((plus(a[0], b[0]), minus(a[1], b[1])))
        odd.append(turn((minus(a[0], b[0]), plus(a[1], b[1])), k, count, 1.0))
    if half == 1:
        even = [(spec[0][0] + spec[1][0], None)]
        odd = [(spec[0][0] - spec[1][0], None)]
    out = [None] * count
    out[0::2] = small_irfft(even, half)
    out[1::2] = small_irfft(odd, half)
    return out


def tables(outer):
    length = outer * INNER
    j = np.arange(INNER)
    k = np.arange(outer // 2 + 1)
    inner = 2.0 * np.pi * (np.outer(j, j) % INNER) / INNER
    c, s = np.cos(inner), np.sin(inner)
    forward = np.block([[c, -s], [s, c]])
    backward = np.block([[c, s], [-s, c]])
    twist = 2.0 * np.pi * (np.outer(k, j) % length) / length
    return forward, backward, np.cos(twist), np.sin(twist)


MESH = pl.DeviceIdType.MESH
MIXED, GATED, TAPS, CONV, CORR, FSUM, SKIP = range(7)


def split(x):
    high = x.astype(jnp.bfloat16)
    return high, (x - high.astype(jnp.float32)).astype(jnp.bfloat16)


def kernel(
    shards, groups, gate_in, out_gate, value_in, out_grad, skip_gain, taps, fwd_hi, fwd_lo,
    bwd_hi, bwd_lo, cos_t, sin_t, grad_gate, grad_out_gate, grad_value, skip_grad, taps_grad,
    sbuf, rbuf, a_hi, a_lo, spec, wide, obuf, nbuf, fbuf, zbuf, fsum, frecv, tbuf, kbuf, krecv,
    send_sem, recv_sem, zsend_sem, zrecv_sem,
):
    f32 = jnp.float32
    rows, channels = gate_in.shape
    own = channels // shards
    width = own // groups
    pieces = rows // INNER
    blocks = shards * pieces
    outer = 2 * blocks
    half = outer // 2 + 1
    length = outer * INNER
    me = lax.axis_index("seq")
    zme = lax.axis_index("chan")

    def peer(d):
        return lax.rem(me + d, shards)

    def zpeer(d):
        return lax.rem(zme + d, groups)

    def each(count, fn):
        def step(d, carry):
            fn(d)
            return carry

        lax.fori_loop(1, count, step, 0)

    def copy(slot, src, dst, to, source):
        return pltpu.make_async_remote_copy(
            src_ref=src, dst_ref=dst, send_sem=send_sem.at[slot, to],
            recv_sem=recv_sem.at[slot, source], device_id={"seq": to}, device_id_type=MESH,
        )

    def zcopy(slot, src, dst, to, source):
        return pltpu.make_async_remote_copy(
            src_ref=src, dst_ref=dst, send_sem=zsend_sem.at[slot, to],
            recv_sem=zrecv_sem.at[slot, source], device_id={"chan": to}, device_id_type=MESH,
        )

    places = {
        MIXED: (lambda p: sbuf.at[0, p], lambda q: rbuf.at[0, q]),
        GATED: (lambda p: sbuf.at[1, p], lambda q: rbuf.at[1, q]),
        TAPS: (lambda p: sbuf.at[2, p], lambda q: rbuf.at[2, q]),
        CONV: (lambda p: obuf.at[0, p], lambda q: nbuf.at[0, q]),
        CORR: (lambda p: obuf.at[1, p], lambda q: nbuf.at[1, q]),
        FSUM: (lambda p: fsum.at[p], lambda q: frecv.at[q]),
        SKIP: (lambda p: kbuf, lambda q: krecv.at[q]),
    }
    zplaces = [
        (lambda p: fbuf.at[p], lambda q: zbuf.at[q]),
        (lambda p: frecv, lambda q: tbuf.at[q]),
    ]

    def send(slot):
        src, dst = places[slot]
        each(shards, lambda d: copy(slot, src(peer(d)), dst(me), peer(d), me).start())

    def arrive(slot):
        dst = places[slot][1]
        each(
            shards,
            lambda d: copy(slot, dst(peer(d)), dst(peer(d)), peer(d), peer(d)).wait_recv(),
        )

    def sent(slot):
        src, dst = places[slot]
        each(shards, lambda d: copy(slot, src(peer(d)), dst(me), peer(d), me).wait_send())

    def zsend(slot):
        src, dst = zplaces[slot]
        each(groups, lambda d: zcopy(slot, src(zpeer(d)), dst(zme), zpeer(d), zme).start())

    def zarrive(slot):
        dst = zplaces[slot][1]
        each(
            groups,
            lambda d: zcopy(slot, dst(zpeer(d)), dst(zpeer(d)), zpeer(d), zpeer(d)).wait_recv(),
        )

    def zsent(slot):
        src, dst = zplaces[slot]
        each(groups, lambda d: zcopy(slot, src(zpeer(d)), dst(zme), zpeer(d), zme).wait_send())

    barrier = pltpu.get_barrier_semaphore()
    each(
        shards,
        lambda d: pl.semaphore_signal(
            barrier, inc=1, device_id={"seq": peer(d)}, device_id_type=MESH
        ),
    )
    each(
        groups,
        lambda d: pl.semaphore_signal(
            barrier, inc=1, device_id={"chan": zpeer(d)}, device_id_type=MESH
        ),
    )

    def product(a, b, at):
        x = a[:, at : at + 128].astype(f32) * b[:, at : at + 128].astype(f32)
        return x.astype(jnp.bfloat16).astype(f32)

    per = 128 // own

    def put(field, at, value):
        sbuf[field, at // own : at // own + per] = value.T.reshape(per, own, rows)

    def keep(field):
        rbuf[field, me] = sbuf[field, me]

    for at in range(0, channels, 128):
        put(0, at, product(gate_in, value_in, at))
    pl.semaphore_wait(barrier, shards - 1 + groups - 1)
    send(MIXED)
    for at in range(0, channels, 128):
        put(1, at, product(out_grad, out_gate, at))
    send(GATED)
    for at in range(0, channels, 128):
        put(2, at, taps[:, at : at + 128])
    send(TAPS)
    for at in range(0, channels, 128):
        both = product(gate_in, value_in, at) * product(out_grad, out_gate, at)
        kbuf[:, at : at + 128] = jnp.sum(both.reshape(rows // 8, 8, 128), axis=0)
    send(SKIP)
    krecv[me] = kbuf[...]
    for field in range(3):
        keep(field)

    def forward(field):
        def tile(g, carry):
            at = pl.ds(pl.multiple_of(g * 16, 16), 16)
            for lane in range(0, INNER, 128):
                series = []
                for i in range(blocks):
                    low = (i % pieces) * INNER + lane
                    series.append(rbuf[field, i // pieces, at, low : low + 128])
                for k, (re, im) in enumerate(small_rfft(series + [None] * blocks)):
                    c = cos_t[k : k + 1, lane : lane + 128]
                    s = sin_t[k : k + 1, lane : lane + 128]
                    tr = re * c if im is None else re * c + im * s
                    ti = -(re * s) if im is None else im * c - re * s
                    for z, low in ((tr, lane), (ti, INNER + lane)):
                        high, rest = split(z)
                        a_hi[k, at, low : low + 128] = high
                        a_lo[k, at, low : low + 128] = rest
            return carry

        lax.fori_loop(0, own // 16, tile, 0)
        spec[field] = times(fwd_hi, fwd_lo)

    def times(hi, lo):
        ah = a_hi[...].reshape(half * own, 2 * INNER)
        al = a_lo[...].reshape(half * own, 2 * INNER)
        out = jnp.dot(ah, hi[...], preferred_element_type=f32)
        out += jnp.dot(al, hi[...], preferred_element_type=f32)
        out += jnp.dot(ah, lo[...], preferred_element_type=f32)
        return out.reshape(half, own, 2 * INNER)

    def backward(first, second, conjugate, store):
        def multiply(k, carry):
            ar, ai = spec[first, k, :, :INNER], spec[first, k, :, INNER:]
            br, bi = spec[second, k, :, :INNER], spec[second, k, :, INNER:]
            if conjugate:
                re, im = ar * br + ai * bi, ai * br - ar * bi
            else:
                re, im = ar * br - ai * bi, ar * bi + ai * br
            high, rest = split(re)
            a_hi[k, :, :INNER] = high
            a_lo[k, :, :INNER] = rest
            high, rest = split(im)
            a_hi[k, :, INNER:] = high
            a_lo[k, :, INNER:] = rest
            return carry

        lax.fori_loop(0, half, multiply, 0)
        wide[...] = times(bwd_hi, bwd_lo)

        def tile(g, carry):
            at = pl.ds(pl.multiple_of(g * 8, 8), 8)
            for lane in range(0, INNER, 128):
                items = []
                for k in range(half):
                    br = wide[k, at, lane : lane + 128]
                    bi = wide[k, at, INNER + lane : INNER + lane + 128]
                    c = cos_t[k : k + 1, lane : lane + 128] * (1.0 / length)
                    s = sin_t[k : k + 1, lane : lane + 128] * (1.0 / length)
                    items.append((br * c - bi * s, bi * c + br * s))
                out = small_irfft(items, outer)
                for i in range(blocks):
                    store(g, i // pieces, (i % pieces) * INNER + lane, out[i])
            return carry

        lax.fori_loop(0, own // 8, tile, 0)

    def store_in(field):
        def store(g, block, low, value):
            at = pl.ds(pl.multiple_of(g * 8, 8), 8)
            obuf[field, block, at, low : low + 128] = value

        return store

    def store_filter(g, block, low, value):
        for u in range(8 // width):
            part = value[u * width : (u + 1) * width]
            fbuf[g * (8 // width) + u, block, :, low : low + 128] = part

    arrive(MIXED)
    forward(0)
    arrive(GATED)
    forward(1)
    backward(1, 0, True, store_filter)
    zsend(0)
    zbuf[zme] = fbuf[zme]
    arrive(TAPS)
    forward(2)
    backward(2, 0, False, store_in(0))
    send(CONV)
    nbuf[0, me] = obuf[0, me]
    zarrive(0)
    total = zbuf[0]
    for z in range(1, groups):
        total = total + zbuf[z]
    fsum[...] = total
    send(FSUM)
    frecv[me] = fsum[me]
    backward(1, 2, True, store_in(1))
    send(CORR)
    nbuf[1, me] = obuf[1, me]
    arrive(FSUM)
    zsend(1)
    tbuf[zme] = frecv[...]
    arrive(SKIP)
    skips = krecv[0]
    for q in range(1, shards):
        skips = skips + krecv[q]
    skip_grad[...] = jnp.sum(skips, axis=0, keepdims=True)

    def natural(field, at):
        first = at // own
        return nbuf[field, first : first + per].reshape(128, rows).T

    arrive(CONV)
    for at in range(0, channels, 128):
        cols = slice(at, at + 128)
        mixed = product(gate_in, value_in, at)
        inner = natural(0, at) + skip_gain[:, cols] * mixed
        grad_out_gate[:, cols] = (out_grad[:, cols].astype(f32) * inner).astype(jnp.bfloat16)
    arrive(CORR)
    for at in range(0, channels, 128):
        cols = slice(at, at + 128)
        mix_grad = natural(1, at) + skip_gain[:, cols] * product(out_grad, out_gate, at)
        grad_gate[:, cols] = (mix_grad * value_in[:, cols].astype(f32)).astype(jnp.bfloat16)
        grad_value[:, cols] = (mix_grad * gate_in[:, cols].astype(f32)).astype(jnp.bfloat16)
    zarrive(1)
    for at in range(0, channels, 128):
        parts = [
            tbuf[z, q]
            for q in range(at // own, at // own + per)
            for z in range(groups)
        ]
        taps_grad[:, at : at + 128] = jnp.concatenate(parts, axis=0).T
    for slot in range(7):
        sent(slot)
    for slot in range(2):
        zsent(slot)


def body(gate_in, out_gate, value_in, out_grad, skip_gain, filter_taps):
    f32, bf16 = jnp.float32, jnp.bfloat16
    shards = lax.axis_size("seq")
    groups = lax.axis_size("chan")
    rows, channels = gate_in.shape
    own = channels // shards
    width = own // groups
    outer = 2 * shards * (rows // INNER)
    half = outer // 2 + 1
    forward, backward, cos_t, sin_t = tables(outer)
    mats = []
    for m in (forward, backward):
        high = m.astype(bf16)
        mats += [jnp.asarray(high), jnp.asarray((m - high.astype(np.float64)).astype(bf16))]
    vmem = pl.BlockSpec(memory_space=pltpu.VMEM)
    outs = pl.pallas_call(
        functools.partial(kernel, shards, groups),
        out_shape=(
            jax.ShapeDtypeStruct((rows, channels), bf16),
            jax.ShapeDtypeStruct((rows, channels), bf16),
            jax.ShapeDtypeStruct((rows, channels), bf16),
            jax.ShapeDtypeStruct((1, channels), f32),
            jax.ShapeDtypeStruct((rows, channels), f32),
        ),
        in_specs=[vmem] * 12,
        out_specs=(vmem,) * 5,
        scratch_shapes=[
            pltpu.VMEM((3, shards, own, rows), f32),
            pltpu.VMEM((3, shards, own, rows), f32),
            pltpu.VMEM((half, own, 2 * INNER), bf16),
            pltpu.VMEM((half, own, 2 * INNER), bf16),
            pltpu.VMEM((3, half, own, 2 * INNER), f32),
            pltpu.VMEM((half, own, 2 * INNER), f32),
            pltpu.VMEM((2, shards, own, rows), f32),
            pltpu.VMEM((2, shards, own, rows), f32),
            pltpu.VMEM((groups, shards, width, rows), f32),
            pltpu.VMEM((groups, shards, width, rows), f32),
            pltpu.VMEM((shards, width, rows), f32),
            pltpu.VMEM((shards, width, rows), f32),
            pltpu.VMEM((groups, shards, width, rows), f32),
            pltpu.VMEM((8, channels), f32),
            pltpu.VMEM((shards, 8, channels), f32),
            pltpu.SemaphoreType.DMA((7, shards)),
            pltpu.SemaphoreType.DMA((7, shards)),
            pltpu.SemaphoreType.DMA((2, groups)),
            pltpu.SemaphoreType.DMA((2, groups)),
        ],
        compiler_params=pltpu.CompilerParams(
            collective_id=0, has_side_effects=True, vmem_limit_bytes=50 * 2**20
        ),
        name="hyena",
    )(
        gate_in, out_gate, value_in, out_grad, skip_gain.reshape(1, channels), filter_taps,
        *mats, jnp.asarray(cos_t, f32), jnp.asarray(sin_t, f32),
    )
    return (outs[0], outs[1], outs[2], outs[3].reshape(channels), outs[4])


def solution(mesh):
    wide = P("seq", "chan")
    return jax.shard_map(
        body,
        mesh=mesh,
        in_specs=(wide, wide, wide, wide, P("chan"), P("seq", None)),
        out_specs=(wide, wide, wide, P("chan"), P("seq", None)),
        check_vma=False,
    )
```

```python
import functools
import math

import jax
import jax.numpy as jnp
import numpy as np
from jax import lax
from jax.experimental import pallas as pl
from jax.experimental.pallas import tpu as pltpu
from jax.sharding import PartitionSpec as P

INNER = 256


def scaled(x, factor):
    if x is None or factor == 0.0:
        return None
    if factor == 1.0:
        return x
    if factor == -1.0:
        return -x
    return x * factor


def plus(a, b):
    if a is None:
        return b
    if b is None:
        return a
    return a + b


def minus(a, b):
    if b is None:
        return a
    if a is None:
        return -b
    return a - b


def turn(z, index, count, sign):
    re, im = z
    quarter = {0: (1.0, 0.0), 1: (0.0, 1.0), 2: (-1.0, 0.0), 3: (0.0, -1.0)}
    if 4 * index % count == 0:
        cos_v, sin_v = quarter[4 * index // count % 4]
    else:
        cos_v = math.cos(2.0 * math.pi * index / count)
        sin_v = math.sin(2.0 * math.pi * index / count)
    sin_v *= sign
    return (
        minus(scaled(re, cos_v), scaled(im, sin_v)),
        plus(scaled(im, cos_v), scaled(re, sin_v)),
    )


def small_rfft(rows):
    count = len(rows)
    if count == 1:
        return [(rows[0], None)]
    even = small_rfft(rows[0::2])
    odd = small_rfft(rows[1::2])
    out = [None] * (count // 2 + 1)
    for k in range(count // 4 + 1):
        t = turn(odd[k], k, count, -1.0)
        e = even[k]
        out[k] = (plus(e[0], t[0]), plus(e[1], t[1]))
        if count // 2 - k != k:
            out[count // 2 - k] = (minus(e[0], t[0]), minus(t[1], e[1]))
    return out


def small_irfft(spec, count):
    if count == 1:
        return [spec[0][0]]
    half = count // 2
    even, odd = [], []
    for k in range(count // 4 + 1):
        a, b = spec[k], spec[half - k]
        even.append((plus(a[0], b[0]), minus(a[1], b[1])))
        odd.append(turn((minus(a[0], b[0]), plus(a[1], b[1])), k, count, 1.0))
    if half == 1:
        even = [(spec[0][0] + spec[1][0], None)]
        odd = [(spec[0][0] - spec[1][0], None)]
    out = [None] * count
    out[0::2] = small_irfft(even, half)
    out[1::2] = small_irfft(odd, half)
    return out


def tables(outer):
    length = outer * INNER
    j = np.arange(INNER)
    k = np.arange(outer // 2 + 1)
    inner = 2.0 * np.pi * (np.outer(j, j) % INNER) / INNER
    c, s = np.cos(inner), np.sin(inner)
    forward = np.block([[c, -s], [s, c]])
    backward = np.block([[c, s], [-s, c]])
    twist = 2.0 * np.pi * (np.outer(k, j) % length) / length
    return forward, backward, np.cos(twist), np.sin(twist)


MESH = pl.DeviceIdType.MESH
LOAD_ORDER = (0, 2, 1, 3, 5, 10, 11, 6, 7, 8, 9, 4)
MIXED, GATED, TAPS, CONV, CORR, FSUM, SKIP = range(7)


def split(x):
    high = x.astype(jnp.bfloat16)
    return high, (x - high.astype(jnp.float32)).astype(jnp.bfloat16)


def kernel(
    shards, groups, *refs,
):
    given, refs = refs[:12], refs[12:]
    (
        grad_gate, grad_out_gate, grad_value, skip_grad, taps_grad, load_sem, gate_in, out_gate,
        value_in, out_grad, skip_gain, taps, fwd_hi, fwd_lo, bwd_hi, bwd_lo, cos_t, sin_t, sbuf, rbuf, a_hi, a_lo, spec, wide, obuf, nbuf, fbuf, zbuf, fsum, frecv, tbuf, kbuf, krecv,
        send_sem, recv_sem, zsend_sem, zrecv_sem,
    ) = refs
    held = (
        gate_in, out_gate, value_in, out_grad, skip_gain, taps, fwd_hi, fwd_lo, bwd_hi, bwd_lo,
        cos_t, sin_t,
    )
    loads = [
        pltpu.make_async_copy(given[i], held[i], load_sem.at[i]) for i in range(len(given))
    ]
    for i in LOAD_ORDER:
        loads[i].start()
    f32 = jnp.float32
    rows, channels = gate_in.shape
    own = channels // shards
    width = own // groups
    pieces = rows // INNER
    blocks = shards * pieces
    outer = 2 * blocks
    half = outer // 2 + 1
    length = outer * INNER
    me = lax.axis_index("seq")
    zme = lax.axis_index("chan")

    def peer(d):
        return lax.rem(me + d, shards)

    def zpeer(d):
        return lax.rem(zme + d, groups)

    def each(count, fn):
        def step(d, carry):
            fn(d)
            return carry

        lax.fori_loop(1, count, step, 0)

    def copy(slot, src, dst, to, source):
        return pltpu.make_async_remote_copy(
            src_ref=src, dst_ref=dst, send_sem=send_sem.at[slot, to],
            recv_sem=recv_sem.at[slot, source], device_id={"seq": to}, device_id_type=MESH,
        )

    def zcopy(slot, src, dst, to, source):
        return pltpu.make_async_remote_copy(
            src_ref=src, dst_ref=dst, send_sem=zsend_sem.at[slot, to],
            recv_sem=zrecv_sem.at[slot, source], device_id={"chan": to}, device_id_type=MESH,
        )

    places = {
        MIXED: (lambda p: sbuf.at[0, p], lambda q: rbuf.at[0, q]),
        GATED: (lambda p: sbuf.at[1, p], lambda q: rbuf.at[1, q]),
        TAPS: (lambda p: sbuf.at[2, p], lambda q: rbuf.at[2, q]),
        CONV: (lambda p: obuf.at[0, p], lambda q: nbuf.at[0, q]),
        CORR: (lambda p: obuf.at[1, p], lambda q: nbuf.at[1, q]),
        FSUM: (lambda p: fsum.at[p], lambda q: frecv.at[q]),
        SKIP: (lambda p: kbuf, lambda q: krecv.at[q]),
    }
    zplaces = [
        (lambda p: fbuf.at[p], lambda q: zbuf.at[q]),
        (lambda p: frecv, lambda q: tbuf.at[q]),
    ]

    def send(slot):
        src, dst = places[slot]
        each(shards, lambda d: copy(slot, src(peer(d)), dst(me), peer(d), me).start())

    def arrive(slot):
        dst = places[slot][1]
        each(
            shards,
            lambda d: copy(slot, dst(peer(d)), dst(peer(d)), peer(d), peer(d)).wait_recv(),
        )

    def sent(slot):
        src, dst = places[slot]
        each(shards, lambda d: copy(slot, src(peer(d)), dst(me), peer(d), me).wait_send())

    def zsend(slot):
        src, dst = zplaces[slot]
        each(groups, lambda d: zcopy(slot, src(zpeer(d)), dst(zme), zpeer(d), zme).start())

    def zarrive(slot):
        dst = zplaces[slot][1]
        each(
            groups,
            lambda d: zcopy(slot, dst(zpeer(d)), dst(zpeer(d)), zpeer(d), zpeer(d)).wait_recv(),
        )

    def zsent(slot):
        src, dst = zplaces[slot]
        each(groups, lambda d: zcopy(slot, src(zpeer(d)), dst(zme), zpeer(d), zme).wait_send())

    barrier = pltpu.get_barrier_semaphore()
    each(
        shards,
        lambda d: pl.semaphore_signal(
            barrier, inc=1, device_id={"seq": peer(d)}, device_id_type=MESH
        ),
    )
    each(
        groups,
        lambda d: pl.semaphore_signal(
            barrier, inc=1, device_id={"chan": zpeer(d)}, device_id_type=MESH
        ),
    )

    def product(a, b, at):
        x = a[:, at : at + 128].astype(f32) * b[:, at : at + 128].astype(f32)
        return x.astype(jnp.bfloat16).astype(f32)

    per = 128 // own

    def put(field, at, value):
        sbuf[field, at // own : at // own + per] = value.T.reshape(per, own, rows)

    def keep(field):
        rbuf[field, me] = sbuf[field, me]

    loads[0].wait()
    loads[2].wait()
    for at in range(0, channels, 128):
        put(0, at, product(gate_in, value_in, at))
    pl.semaphore_wait(barrier, shards - 1 + groups - 1)
    send(MIXED)
    loads[1].wait()
    loads[3].wait()
    for at in range(0, channels, 128):
        put(1, at, product(out_grad, out_gate, at))
    send(GATED)
    loads[5].wait()
    for at in range(0, channels, 128):
        put(2, at, taps[:, at : at + 128])
    send(TAPS)
    for at in range(0, channels, 128):
        both = product(gate_in, value_in, at) * product(out_grad, out_gate, at)
        kbuf[:, at : at + 128] = jnp.sum(both.reshape(rows // 8, 8, 128), axis=0)
    send(SKIP)
    krecv[me] = kbuf[...]
    for field in range(3):
        keep(field)

    def forward(field):
        def tile(g, carry):
            at = pl.ds(pl.multiple_of(g * 16, 16), 16)
            for lane in range(0, INNER, 128):
                series = []
                for i in range(blocks):
                    low = (i % pieces) * INNER + lane
                    series.append(rbuf[field, i // pieces, at, low : low + 128])
                for k, (re, im) in enumerate(small_rfft(series + [None] * blocks)):
                    c = cos_t[k : k + 1, lane : lane + 128]
                    s = sin_t[k : k + 1, lane : lane + 128]
                    tr = re * c if im is None else re * c + im * s
                    ti = -(re * s) if im is None else im * c - re * s
                    for z, low in ((tr, lane), (ti, INNER + lane)):
                        high, rest = split(z)
                        a_hi[k, at, low : low + 128] = high
                        a_lo[k, at, low : low + 128] = rest
            return carry

        lax.fori_loop(0, own // 16, tile, 0)
        spec[field] = times(fwd_hi, fwd_lo)

    def times(hi, lo):
        ah = a_hi[...].reshape(half * own, 2 * INNER)
        al = a_lo[...].reshape(half * own, 2 * INNER)
        out = jnp.dot(ah, hi[...], preferred_element_type=f32)
        out += jnp.dot(al, hi[...], preferred_element_type=f32)
        out += jnp.dot(ah, lo[...], preferred_element_type=f32)
        return out.reshape(half, own, 2 * INNER)

    def backward(first, second, conjugate, store):
        def multiply(k, carry):
            ar, ai = spec[first, k, :, :INNER], spec[first, k, :, INNER:]
            br, bi = spec[second, k, :, :INNER], spec[second, k, :, INNER:]
            if conjugate:
                re, im = ar * br + ai * bi, ai * br - ar * bi
            else:
                re, im = ar * br - ai * bi, ar * bi + ai * br
            high, rest = split(re)
            a_hi[k, :, :INNER] = high
            a_lo[k, :, :INNER] = rest
            high, rest = split(im)
            a_hi[k, :, INNER:] = high
            a_lo[k, :, INNER:] = rest
            return carry

        lax.fori_loop(0, half, multiply, 0)
        wide[...] = times(bwd_hi, bwd_lo)

        def tile(g, carry):
            at = pl.ds(pl.multiple_of(g * 8, 8), 8)
            for lane in range(0, INNER, 128):
                items = []
                for k in range(half):
                    br = wide[k, at, lane : lane + 128]
                    bi = wide[k, at, INNER + lane : INNER + lane + 128]
                    c = cos_t[k : k + 1, lane : lane + 128] * (1.0 / length)
                    s = sin_t[k : k + 1, lane : lane + 128] * (1.0 / length)
                    items.append((br * c - bi * s, bi * c + br * s))
                out = small_irfft(items, outer)
                for i in range(blocks):
                    store(g, i // pieces, (i % pieces) * INNER + lane, out[i])
            return carry

        lax.fori_loop(0, own // 8, tile, 0)

    def store_in(field):
        def store(g, block, low, value):
            at = pl.ds(pl.multiple_of(g * 8, 8), 8)
            obuf[field, block, at, low : low + 128] = value

        return store

    def store_filter(g, block, low, value):
        for u in range(8 // width):
            part = value[u * width : (u + 1) * width]
            fbuf[g * (8 // width) + u, block, :, low : low + 128] = part

    for i in (10, 11, 6, 7, 8, 9, 4):
        loads[i].wait()
    arrive(MIXED)
    forward(0)
    arrive(GATED)
    forward(1)
    backward(1, 0, True, store_filter)
    zsend(0)
    zbuf[zme] = fbuf[zme]
    arrive(TAPS)
    forward(2)
    backward(2, 0, False, store_in(0))
    send(CONV)
    nbuf[0, me] = obuf[0, me]
    zarrive(0)
    total = zbuf[0]
    for z in range(1, groups):
        total = total + zbuf[z]
    fsum[...] = total
    send(FSUM)
    frecv[me] = fsum[me]
    backward(1, 2, True, store_in(1))
    send(CORR)
    nbuf[1, me] = obuf[1, me]
    arrive(FSUM)
    zsend(1)
    tbuf[zme] = frecv[...]
    arrive(SKIP)
    skips = krecv[0]
    for q in range(1, shards):
        skips = skips + krecv[q]
    skip_grad[...] = jnp.sum(skips, axis=0, keepdims=True)

    def natural(field, at):
        first = at // own
        return nbuf[field, first : first + per].reshape(128, rows).T

    arrive(CONV)
    for at in range(0, channels, 128):
        cols = slice(at, at + 128)
        mixed = product(gate_in, value_in, at)
        inner = natural(0, at) + skip_gain[:, cols] * mixed
        grad_out_gate[:, cols] = (out_grad[:, cols].astype(f32) * inner).astype(jnp.bfloat16)
    arrive(CORR)
    for at in range(0, channels, 128):
        cols = slice(at, at + 128)
        mix_grad = natural(1, at) + skip_gain[:, cols] * product(out_grad, out_gate, at)
        grad_gate[:, cols] = (mix_grad * value_in[:, cols].astype(f32)).astype(jnp.bfloat16)
        grad_value[:, cols] = (mix_grad * gate_in[:, cols].astype(f32)).astype(jnp.bfloat16)
    zarrive(1)
    for at in range(0, channels, 128):
        parts = [
            tbuf[z, q]
            for q in range(at // own, at // own + per)
            for z in range(groups)
        ]
        taps_grad[:, at : at + 128] = jnp.concatenate(parts, axis=0).T
    for slot in range(7):
        sent(slot)
    for slot in range(2):
        zsent(slot)


def body(gate_in, out_gate, value_in, out_grad, skip_gain, filter_taps):
    f32, bf16 = jnp.float32, jnp.bfloat16
    shards = lax.axis_size("seq")
    groups = lax.axis_size("chan")
    rows, channels = gate_in.shape
    own = channels // shards
    width = own // groups
    outer = 2 * shards * (rows // INNER)
    half = outer // 2 + 1
    forward, backward, cos_t, sin_t = tables(outer)
    mats = []
    for m in (forward, backward):
        high = m.astype(bf16)
        mats += [jnp.asarray(high), jnp.asarray((m - high.astype(np.float64)).astype(bf16))]
    inputs = (
        gate_in, out_gate, value_in, out_grad, skip_gain.reshape(1, channels), filter_taps,
        *mats, jnp.asarray(cos_t, f32), jnp.asarray(sin_t, f32),
    )
    vmem = pl.BlockSpec(memory_space=pltpu.VMEM)
    outs = pl.pallas_call(
        functools.partial(kernel, shards, groups),
        out_shape=(
            jax.ShapeDtypeStruct((rows, channels), bf16),
            jax.ShapeDtypeStruct((rows, channels), bf16),
            jax.ShapeDtypeStruct((rows, channels), bf16),
            jax.ShapeDtypeStruct((1, channels), f32),
            jax.ShapeDtypeStruct((rows, channels), f32),
        ),
        in_specs=[pl.BlockSpec(memory_space=pltpu.HBM)] * 12,
        out_specs=(vmem,) * 5,
        scratch_shapes=[pltpu.SemaphoreType.DMA((12,))]
        + [pltpu.VMEM(x.shape, x.dtype) for x in inputs]
        + [
            pltpu.VMEM((3, shards, own, rows), f32),
            pltpu.VMEM((3, shards, own, rows), f32),
            pltpu.VMEM((half, own, 2 * INNER), bf16),
            pltpu.VMEM((half, own, 2 * INNER), bf16),
            pltpu.VMEM((3, half, own, 2 * INNER), f32),
            pltpu.VMEM((half, own, 2 * INNER), f32),
            pltpu.VMEM((2, shards, own, rows), f32),
            pltpu.VMEM((2, shards, own, rows), f32),
            pltpu.VMEM((groups, shards, width, rows), f32),
            pltpu.VMEM((groups, shards, width, rows), f32),
            pltpu.VMEM((shards, width, rows), f32),
            pltpu.VMEM((shards, width, rows), f32),
            pltpu.VMEM((groups, shards, width, rows), f32),
            pltpu.VMEM((8, channels), f32),
            pltpu.VMEM((shards, 8, channels), f32),
            pltpu.SemaphoreType.DMA((7, shards)),
            pltpu.SemaphoreType.DMA((7, shards)),
            pltpu.SemaphoreType.DMA((2, groups)),
            pltpu.SemaphoreType.DMA((2, groups)),
        ],
        compiler_params=pltpu.CompilerParams(
            collective_id=0, has_side_effects=True, vmem_limit_bytes=60 * 2**20
        ),
        name="hyena",
    )(*inputs)
    return (outs[0], outs[1], outs[2], outs[3].reshape(channels), outs[4])


def solution(mesh):
    wide = P("seq", "chan")
    return jax.shard_map(
        body,
        mesh=mesh,
        in_specs=(wide, wide, wide, wide, P("chan"), P("seq", None)),
        out_specs=(wide, wide, wide, P("chan"), P("seq", None)),
        check_vma=False,
    )
```

```python
import functools
import math

import jax
import jax.numpy as jnp
import numpy as np
from jax import lax
from jax.experimental import pallas as pl
from jax.experimental.pallas import tpu as pltpu
from jax.sharding import PartitionSpec as P

INNER = 256


def scaled(x, factor):
    if x is None or factor == 0.0:
        return None
    if factor == 1.0:
        return x
    if factor == -1.0:
        return -x
    return x * factor


def plus(a, b):
    if a is None:
        return b
    if b is None:
        return a
    return a + b


def minus(a, b):
    if b is None:
        return a
    if a is None:
        return -b
    return a - b


def turn(z, index, count, sign):
    re, im = z
    quarter = {0: (1.0, 0.0), 1: (0.0, 1.0), 2: (-1.0, 0.0), 3: (0.0, -1.0)}
    if 4 * index % count == 0:
        cos_v, sin_v = quarter[4 * index // count % 4]
    else:
        cos_v = math.cos(2.0 * math.pi * index / count)
        sin_v = math.sin(2.0 * math.pi * index / count)
    sin_v *= sign
    return (
        minus(scaled(re, cos_v), scaled(im, sin_v)),
        plus(scaled(im, cos_v), scaled(re, sin_v)),
    )


def small_rfft(rows):
    count = len(rows)
    if count == 1:
        return [(rows[0], None)]
    even = small_rfft(rows[0::2])
    odd = small_rfft(rows[1::2])
    out = [None] * (count // 2 + 1)
    for k in range(count // 4 + 1):
        t = turn(odd[k], k, count, -1.0)
        e = even[k]
        out[k] = (plus(e[0], t[0]), plus(e[1], t[1]))
        if count // 2 - k != k:
            out[count // 2 - k] = (minus(e[0], t[0]), minus(t[1], e[1]))
    return out


def small_irfft(spec, count):
    if count == 1:
        return [spec[0][0]]
    half = count // 2
    even, odd = [], []
    for k in range(count // 4 + 1):
        a, b = spec[k], spec[half - k]
        even.append((plus(a[0], b[0]), minus(a[1], b[1])))
        odd.append(turn((minus(a[0], b[0]), plus(a[1], b[1])), k, count, 1.0))
    if half == 1:
        even = [(spec[0][0] + spec[1][0], None)]
        odd = [(spec[0][0] - spec[1][0], None)]
    out = [None] * count
    out[0::2] = small_irfft(even, half)
    out[1::2] = small_irfft(odd, half)
    return out


def tables(outer):
    length = outer * INNER
    j = np.arange(INNER)
    k = np.arange(outer // 2 + 1)
    inner = 2.0 * np.pi * (np.outer(j, j) % INNER) / INNER
    c, s = np.cos(inner), np.sin(inner)
    forward = np.block([[c, -s], [s, c]])
    backward = np.block([[c, s], [-s, c]])
    twist = 2.0 * np.pi * (np.outer(k, j) % length) / length
    return forward, backward, np.cos(twist), np.sin(twist)


MESH = pl.DeviceIdType.MESH
LOAD_ORDER = (0, 2, 1, 3, 5, 10, 11, 6, 7, 8, 9, 4)
MIXED, GATED, TAPS, CONV, CORR, FSUM, SKIP = range(7)


def split(x):
    high = x.astype(jnp.bfloat16)
    return high, (x - high.astype(jnp.float32)).astype(jnp.bfloat16)


def kernel(
    shards, groups, *refs,
):
    given, refs = refs[:12], refs[12:]
    (
        grad_gate, grad_out_gate, grad_value, skip_grad, taps_grad, load_sem, gate_in, out_gate,
        value_in, out_grad, skip_gain, taps, fwd_hi, fwd_lo, bwd_hi, bwd_lo, cos_t, sin_t, sbuf, rbuf, a_hi, a_lo, spec, wide, obuf, nbuf, fbuf, zbuf, fsum, frecv, tbuf, kbuf, krecv, tap_out, tap_in, tap_all,
        send_sem, recv_sem, zsend_sem, zrecv_sem,
    ) = refs
    held = (
        gate_in, out_gate, value_in, out_grad, skip_gain, taps, fwd_hi, fwd_lo, bwd_hi, bwd_lo,
        cos_t, sin_t,
    )
    loads = [
        pltpu.make_async_copy(given[i], held[i], load_sem.at[i]) for i in range(len(given))
    ]
    for i in LOAD_ORDER:
        loads[i].start()
    f32 = jnp.float32
    rows, channels = gate_in.shape
    own = channels // shards
    width = own // groups
    pieces = rows // INNER
    blocks = shards * pieces
    outer = 2 * blocks
    half = outer // 2 + 1
    length = outer * INNER
    me = lax.axis_index("seq")
    zme = lax.axis_index("chan")

    def peer(d):
        return lax.rem(me + d, shards)

    def zpeer(d):
        return lax.rem(zme + d, groups)

    def each(count, fn):
        def step(d, carry):
            fn(d)
            return carry

        lax.fori_loop(1, count, step, 0)

    def copy(slot, src, dst, to, source):
        return pltpu.make_async_remote_copy(
            src_ref=src, dst_ref=dst, send_sem=send_sem.at[slot, to],
            recv_sem=recv_sem.at[slot, source], device_id={"seq": to}, device_id_type=MESH,
        )

    def zcopy(slot, src, dst, to, source):
        return pltpu.make_async_remote_copy(
            src_ref=src, dst_ref=dst, send_sem=zsend_sem.at[slot, to],
            recv_sem=zrecv_sem.at[slot, source], device_id={"chan": to}, device_id_type=MESH,
        )

    places = {
        MIXED: (lambda p: sbuf.at[0, p], lambda q: rbuf.at[0, q]),
        GATED: (lambda p: sbuf.at[1, p], lambda q: rbuf.at[1, q]),
        TAPS: (lambda p: tap_out.at[zme, p], lambda q: tap_in.at[q]),
        CONV: (lambda p: obuf.at[0, p], lambda q: nbuf.at[0, q]),
        CORR: (lambda p: obuf.at[1, p], lambda q: nbuf.at[1, q]),
        FSUM: (lambda p: fsum.at[p], lambda q: frecv.at[q]),
        SKIP: (lambda p: kbuf, lambda q: krecv.at[q]),
    }
    zplaces = [
        (lambda p: fbuf.at[p], lambda q: zbuf.at[q]),
        (lambda p: frecv, lambda q: tbuf.at[q]),
        (lambda p: tap_in, lambda q: tap_all.at[q]),
    ]

    def send(slot):
        src, dst = places[slot]
        each(shards, lambda d: copy(slot, src(peer(d)), dst(me), peer(d), me).start())

    def arrive(slot):
        dst = places[slot][1]
        each(
            shards,
            lambda d: copy(slot, dst(peer(d)), dst(peer(d)), peer(d), peer(d)).wait_recv(),
        )

    def sent(slot):
        src, dst = places[slot]
        each(shards, lambda d: copy(slot, src(peer(d)), dst(me), peer(d), me).wait_send())

    def zsend(slot):
        src, dst = zplaces[slot]
        each(groups, lambda d: zcopy(slot, src(zpeer(d)), dst(zme), zpeer(d), zme).start())

    def zarrive(slot):
        dst = zplaces[slot][1]
        each(
            groups,
            lambda d: zcopy(slot, dst(zpeer(d)), dst(zpeer(d)), zpeer(d), zpeer(d)).wait_recv(),
        )

    def zsent(slot):
        src, dst = zplaces[slot]
        each(groups, lambda d: zcopy(slot, src(zpeer(d)), dst(zme), zpeer(d), zme).wait_send())

    barrier = pltpu.get_barrier_semaphore()
    each(
        shards,
        lambda d: pl.semaphore_signal(
            barrier, inc=1, device_id={"seq": peer(d)}, device_id_type=MESH
        ),
    )
    each(
        groups,
        lambda d: pl.semaphore_signal(
            barrier, inc=1, device_id={"chan": zpeer(d)}, device_id_type=MESH
        ),
    )

    def product(a, b, at):
        x = a[:, at : at + 128].astype(f32) * b[:, at : at + 128].astype(f32)
        return x.astype(jnp.bfloat16).astype(f32)

    per = 128 // own

    def put(field, at, value):
        sbuf[field, at // own : at // own + per] = value.T.reshape(per, own, rows)

    def keep(field):
        rbuf[field, me] = sbuf[field, me]

    loads[0].wait()
    loads[2].wait()
    for at in range(0, channels, 128):
        put(0, at, product(gate_in, value_in, at))
    pl.semaphore_wait(barrier, shards - 1 + groups - 1)
    send(MIXED)
    loads[5].wait()
    for at in range(0, channels, 128):
        flipped = taps[:, at : at + 128].T
        for u in range(128 // width):
            row = at + u * width
            tap_out[row % own // width, row // own] = flipped[u * width : (u + 1) * width]
    send(TAPS)
    tap_in[me] = tap_out[zme, me]
    loads[1].wait()
    loads[3].wait()
    for at in range(0, channels, 128):
        put(1, at, product(out_grad, out_gate, at))
    send(GATED)
    for at in range(0, channels, 128):
        both = product(gate_in, value_in, at) * product(out_grad, out_gate, at)
        kbuf[:, at : at + 128] = jnp.sum(both.reshape(rows // 8, 8, 128), axis=0)
    send(SKIP)
    krecv[me] = kbuf[...]
    for field in range(2):
        keep(field)
    arrive(TAPS)
    zsend(2)
    tap_all[zme] = tap_in[...]

    def forward(field):
        def tile(g, carry):
            at = pl.ds(pl.multiple_of(g * 16, 16), 16)
            for lane in range(0, INNER, 128):
                series = []
                for i in range(blocks):
                    low = (i % pieces) * INNER + lane
                    series.append(rbuf[field, i // pieces, at, low : low + 128])
                for k, (re, im) in enumerate(small_rfft(series + [None] * blocks)):
                    c = cos_t[k : k + 1, lane : lane + 128]
                    s = sin_t[k : k + 1, lane : lane + 128]
                    tr = re * c if im is None else re * c + im * s
                    ti = -(re * s) if im is None else im * c - re * s
                    for z, low in ((tr, lane), (ti, INNER + lane)):
                        high, rest = split(z)
                        a_hi[k, at, low : low + 128] = high
                        a_lo[k, at, low : low + 128] = rest
            return carry

        lax.fori_loop(0, own // 16, tile, 0)
        spec[field] = times(fwd_hi, fwd_lo)

    def times(hi, lo):
        ah = a_hi[...].reshape(half * own, 2 * INNER)
        al = a_lo[...].reshape(half * own, 2 * INNER)
        out = jnp.dot(ah, hi[...], preferred_element_type=f32)
        out += jnp.dot(al, hi[...], preferred_element_type=f32)
        out += jnp.dot(ah, lo[...], preferred_element_type=f32)
        return out.reshape(half, own, 2 * INNER)

    def backward(first, second, conjugate, store):
        def multiply(k, carry):
            ar, ai = spec[first, k, :, :INNER], spec[first, k, :, INNER:]
            br, bi = spec[second, k, :, :INNER], spec[second, k, :, INNER:]
            if conjugate:
                re, im = ar * br + ai * bi, ai * br - ar * bi
            else:
                re, im = ar * br - ai * bi, ar * bi + ai * br
            high, rest = split(re)
            a_hi[k, :, :INNER] = high
            a_lo[k, :, :INNER] = rest
            high, rest = split(im)
            a_hi[k, :, INNER:] = high
            a_lo[k, :, INNER:] = rest
            return carry

        lax.fori_loop(0, half, multiply, 0)
        wide[...] = times(bwd_hi, bwd_lo)

        def tile(g, carry):
            at = pl.ds(pl.multiple_of(g * 8, 8), 8)
            for lane in range(0, INNER, 128):
                items = []
                for k in range(half):
                    br = wide[k, at, lane : lane + 128]
                    bi = wide[k, at, INNER + lane : INNER + lane + 128]
                    c = cos_t[k : k + 1, lane : lane + 128] * (1.0 / length)
                    s = sin_t[k : k + 1, lane : lane + 128] * (1.0 / length)
                    items.append((br * c - bi * s, bi * c + br * s))
                out = small_irfft(items, outer)
                for i in range(blocks):
                    store(g, i // pieces, (i % pieces) * INNER + lane, out[i])
            return carry

        lax.fori_loop(0, own // 8, tile, 0)

    def store_in(field):
        def store(g, block, low, value):
            at = pl.ds(pl.multiple_of(g * 8, 8), 8)
            obuf[field, block, at, low : low + 128] = value

        return store

    def store_filter(g, block, low, value):
        for u in range(8 // width):
            part = value[u * width : (u + 1) * width]
            fbuf[g * (8 // width) + u, block, :, low : low + 128] = part

    for i in (10, 11, 6, 7, 8, 9, 4):
        loads[i].wait()
    arrive(MIXED)
    forward(0)
    arrive(GATED)
    forward(1)
    backward(1, 0, True, store_filter)
    zsend(0)
    zbuf[zme] = fbuf[zme]
    zarrive(2)
    for z in range(groups):
        rbuf[2, :, z * width : (z + 1) * width, :] = tap_all[z]
    forward(2)
    backward(2, 0, False, store_in(0))
    send(CONV)
    nbuf[0, me] = obuf[0, me]
    zarrive(0)
    total = zbuf[0]
    for z in range(1, groups):
        total = total + zbuf[z]
    fsum[...] = total
    send(FSUM)
    frecv[me] = fsum[me]
    backward(1, 2, True, store_in(1))
    send(CORR)
    nbuf[1, me] = obuf[1, me]
    arrive(FSUM)
    zsend(1)
    tbuf[zme] = frecv[...]
    arrive(SKIP)
    skips = krecv[0]
    for q in range(1, shards):
        skips = skips + krecv[q]
    skip_grad[...] = jnp.sum(skips, axis=0, keepdims=True)

    def natural(field, at):
        first = at // own
        return nbuf[field, first : first + per].reshape(128, rows).T

    arrive(CONV)
    for at in range(0, channels, 128):
        cols = slice(at, at + 128)
        mixed = product(gate_in, value_in, at)
        inner = natural(0, at) + skip_gain[:, cols] * mixed
        grad_out_gate[:, cols] = (out_grad[:, cols].astype(f32) * inner).astype(jnp.bfloat16)
    arrive(CORR)
    for at in range(0, channels, 128):
        cols = slice(at, at + 128)
        mix_grad = natural(1, at) + skip_gain[:, cols] * product(out_grad, out_gate, at)
        grad_gate[:, cols] = (mix_grad * value_in[:, cols].astype(f32)).astype(jnp.bfloat16)
        grad_value[:, cols] = (mix_grad * gate_in[:, cols].astype(f32)).astype(jnp.bfloat16)
    zarrive(1)
    for at in range(0, channels, 128):
        parts = [
            tbuf[z, q]
            for q in range(at // own, at // own + per)
            for z in range(groups)
        ]
        taps_grad[:, at : at + 128] = jnp.concatenate(parts, axis=0).T
    for slot in range(7):
        sent(slot)
    for slot in range(3):
        zsent(slot)


def body(gate_in, out_gate, value_in, out_grad, skip_gain, filter_taps):
    f32, bf16 = jnp.float32, jnp.bfloat16
    shards = lax.axis_size("seq")
    groups = lax.axis_size("chan")
    rows, channels = gate_in.shape
    own = channels // shards
    width = own // groups
    outer = 2 * shards * (rows // INNER)
    half = outer // 2 + 1
    forward, backward, cos_t, sin_t = tables(outer)
    mats = []
    for m in (forward, backward):
        high = m.astype(bf16)
        mats += [jnp.asarray(high), jnp.asarray((m - high.astype(np.float64)).astype(bf16))]
    inputs = (
        gate_in, out_gate, value_in, out_grad, skip_gain.reshape(1, channels), filter_taps,
        *mats, jnp.asarray(cos_t, f32), jnp.asarray(sin_t, f32),
    )
    vmem = pl.BlockSpec(memory_space=pltpu.VMEM)
    outs = pl.pallas_call(
        functools.partial(kernel, shards, groups),
        out_shape=(
            jax.ShapeDtypeStruct((rows, channels), bf16),
            jax.ShapeDtypeStruct((rows, channels), bf16),
            jax.ShapeDtypeStruct((rows, channels), bf16),
            jax.ShapeDtypeStruct((1, channels), f32),
            jax.ShapeDtypeStruct((rows, channels), f32),
        ),
        in_specs=[pl.BlockSpec(memory_space=pltpu.HBM)] * 12,
        out_specs=(vmem,) * 5,
        scratch_shapes=[pltpu.SemaphoreType.DMA((12,))]
        + [pltpu.VMEM(x.shape, x.dtype) for x in inputs]
        + [
            pltpu.VMEM((3, shards, own, rows), f32),
            pltpu.VMEM((3, shards, own, rows), f32),
            pltpu.VMEM((half, own, 2 * INNER), bf16),
            pltpu.VMEM((half, own, 2 * INNER), bf16),
            pltpu.VMEM((3, half, own, 2 * INNER), f32),
            pltpu.VMEM((half, own, 2 * INNER), f32),
            pltpu.VMEM((2, shards, own, rows), f32),
            pltpu.VMEM((2, shards, own, rows), f32),
            pltpu.VMEM((groups, shards, width, rows), f32),
            pltpu.VMEM((groups, shards, width, rows), f32),
            pltpu.VMEM((shards, width, rows), f32),
            pltpu.VMEM((shards, width, rows), f32),
            pltpu.VMEM((groups, shards, width, rows), f32),
            pltpu.VMEM((8, channels), f32),
            pltpu.VMEM((shards, 8, channels), f32),
            pltpu.VMEM((groups, shards, width, rows), f32),
            pltpu.VMEM((shards, width, rows), f32),
            pltpu.VMEM((groups, shards, width, rows), f32),
            pltpu.SemaphoreType.DMA((7, shards)),
            pltpu.SemaphoreType.DMA((7, shards)),
            pltpu.SemaphoreType.DMA((3, groups)),
            pltpu.SemaphoreType.DMA((3, groups)),
        ],
        compiler_params=pltpu.CompilerParams(
            collective_id=0, has_side_effects=True, vmem_limit_bytes=60 * 2**20
        ),
        name="hyena",
    )(*inputs)
    return (outs[0], outs[1], outs[2], outs[3].reshape(channels), outs[4])


def solution(mesh):
    wide = P("seq", "chan")
    return jax.shard_map(
        body,
        mesh=mesh,
        in_specs=(wide, wide, wide, wide, P("chan"), P("seq", None)),
        out_specs=(wide, wide, wide, P("chan"), P("seq", None)),
        check_vma=False,
    )
```
